512 devices in a mesh: tm: 128 (over z, y, core), rows: 4 (over x).
Axes of the slice: x: 4, y: 8, z: 8, core: 2. Of those that a mesh axis runs over, the one named last changes fastest.
Arguments:
- pivot_blocks: float32 [128, 512, 512], P('tm'), may hold values from -4 to 24, as said below
- lower_blocks: float32 [128, 512, 512], P('tm', None, 'rows'), may hold values from -5 to 0.5
- top_diagonal: float32 [128, 512, 512], P('tm', 'rows'), may hold values from -1 to 2, as said below
- top_coupling: float32 [128, 512, 512], P('tm', 'rows'), may hold values from -3 to 3
Outputs:
- sigma_diagonal: float32 [128, 512, 512], P('tm', 'rows')
- sigma_next: float32 [128, 512, 512], P('tm', 'rows')
- reduced_pivot: float32 [128, 512, 512], P('tm', 'rows')
The draws below stay inside these ranges and needn't reach their ends.
Inputs may be any that keep to these rules, and one draw needn't show every extreme that they name: `pivot_blocks`: each block is symmetric, and the block-tridiagonal matrix with these diagonal blocks and the couplings lower_blocks is positive definite. `top_diagonal`: each block is symmetric.
All inputs are finite; a program needn't handle non-finite values.
Results may differ from the reference program's by a relative error of at most 0.0001.
Values sent between devices are 32-bit elements; how exact they have to be, the bound alone decides.
A program may use at most 64 MiB of HBM per device.

```python
import math
import jax
import jax.numpy as jnp
from jax import lax

B = 512
LEVELS = 2
PARTS_SIZE = 128


def symmetric_noise(key, strength):
    raw_values = jnp.clip(jax.random.normal(key, (PARTS_SIZE, B, B), jnp.float32), -4.0, 4.0)
    return (raw_values + jnp.swapaxes(raw_values, 1, 2)) * (0.5 * strength / jnp.sqrt(B * 1.0))


def field_weights(key):
    base_key = jax.random.fold_in(key, 71)
    mass_key, time_key, cross_key, bond_key = jax.random.split(base_key, 4)
    chain_mask = (jnp.arange(B) < B - 1).astype(jnp.float32)
    masses = jax.random.uniform(mass_key, (PARTS_SIZE, B), jnp.float32, 0.5, 1.0)
    time_low = math.log(1.0)
    time_weights = jnp.exp(jax.random.uniform(time_key, (PARTS_SIZE + 1, B), jnp.float32, time_low, math.log(4.0)))
    cross_weights = jnp.exp(jax.random.uniform(cross_key, (PARTS_SIZE + 1, B), jnp.float32, math.log(0.4), math.log(2.0))) * chain_mask[None, :]
    bond_weights = jnp.exp(jax.random.uniform(bond_key, (PARTS_SIZE, B), jnp.float32, math.log(0.3), math.log(3.0))) * chain_mask[None, :]
    return (masses, time_weights, cross_weights, bond_weights)


def draw_pivot_blocks(key, part):
    masses, time_weights, cross_weights, bond_weights = field_weights(key)
    noise_key = jax.random.fold_in(key, 11)
    cross_here = cross_weights[:PARTS_SIZE]
    cross_after = cross_weights[1:]
    diagonal = masses + time_weights[:PARTS_SIZE] + time_weights[1:] + bond_weights + jnp.roll(bond_weights, 1, axis=1)
    diagonal = diagonal + cross_here + jnp.roll(cross_here, 1, axis=1) + cross_after + jnp.roll(cross_after, 1, axis=1)
    identity = jnp.eye(B, dtype=jnp.float32)
    chain_part = jnp.eye(B, k=1, dtype=jnp.float32)[None] * (-bond_weights)[:, :, None]
    return symmetric_noise(noise_key, 0.05) + identity[None] * diagonal[:, None, :] + chain_part + jnp.swapaxes(chain_part, 1, 2)


def draw_lower_blocks(key, part):
    masses, time_weights, cross_weights, bond_weights = field_weights(key)
    noise_key = jax.random.fold_in(key, 37)
    raw_values = jnp.clip(jax.random.normal(noise_key, (PARTS_SIZE, B, B), jnp.float32), -4.0, 4.0)
    identity = jnp.eye(B, dtype=jnp.float32)
    upper_band = jnp.eye(B, k=1, dtype=jnp.float32)
    cross_here = cross_weights[:PARTS_SIZE]
    coupling = -(identity[None] * time_weights[:PARTS_SIZE][:, None, :])
    coupling = coupling - upper_band[None] * cross_here[:, :, None] - jnp.swapaxes(upper_band, 0, 1)[None] * cross_here[:, None, :]
    return coupling + raw_values * (0.03 / jnp.sqrt(B * 1.0))


def draw_top_diagonal(key, part):
    noise_key, scale_key = jax.random.split(jax.random.fold_in(key, 23))
    scales = jax.random.uniform(scale_key, (PARTS_SIZE, 1, B), jnp.float32, 0.5, 1.5)
    return symmetric_noise(noise_key, 0.5) + jnp.eye(B, dtype=jnp.float32)[None] * scales


def shard_levels(key, dims, cuts, low, top_value):
    def one(position, shards_of):
        heights = jax.random.uniform(jax.random.fold_in(jax.random.fold_in(key, 6), position), (shards_of,), jnp.float32, low / len(cuts), top_value / len(cuts))
        return jnp.repeat(jnp.exp(heights), dims[position] // shards_of).reshape((-1,) + (1,) * (len(dims) - position - 1))

    factor_of = one(*cuts[0])
    for cut in cuts[1:]:
        factor_of = factor_of * one(*cut)
    return factor_of


def scatter_about(stream_key, shape, spread, reach, pieces=(), held_as=jnp.bfloat16):
    values = jax.random.normal(stream_key, shape, jnp.float32) * spread
    if len(pieces) > 0:
        values = shard_levels(stream_key, shape, pieces, -0.22, 0.18) * values
    return jnp.clip(values, min=-reach, max=reach).astype(held_as)


def setup_inputs(seed: int = 0) -> dict:
    keys = jax.random.split(jax.random.key(seed), 5)
    return {
        "pivot_blocks": draw_pivot_blocks(jax.random.fold_in(keys[4], 71), 0),
        "lower_blocks": draw_lower_blocks(jax.random.fold_in(keys[4], 71), 0),
        "top_diagonal": draw_top_diagonal(jax.random.fold_in(keys[4], 71), 0),
        "top_coupling": scatter_about(keys[3], (PARTS_SIZE, B, B), 0.5, 3.0, ((0, 128), (1, 4)), jnp.float32),
    }


precise = lax.Precision.HIGHEST

def batch_product(left, right):
    return jnp.matmul(left, right, precision=precise)

def flipped(blocks):
    return jnp.swapaxes(blocks, 1, 2)

def solve_batch(factor, right_side):
    return jax.vmap(lambda single, given: jax.scipy.linalg.cho_solve((single, True), given))(factor, right_side)

def from_below(blocks, spacing):
    pad_blocks = jnp.zeros((spacing,) + blocks.shape[1:], jnp.float32)
    return jnp.concatenate([pad_blocks, blocks[:-spacing]], 0)

def from_above(blocks, spacing):
    pad_blocks = jnp.zeros((spacing,) + blocks.shape[1:], jnp.float32)
    return jnp.concatenate([blocks[spacing:], pad_blocks], 0)

def reference(pivot_blocks, lower_blocks, top_diagonal, top_coupling):
    parts_count = pivot_blocks.shape[0]
    full_width = pivot_blocks.shape[1]
    indices = jnp.arange(parts_count)
    empty = jnp.zeros((1, full_width, full_width), jnp.float32)
    lower_now = jnp.where((indices == 0)[:, None, None], jnp.float32(0.0), lower_blocks)
    upper_now = jnp.concatenate([flipped(lower_now[1:]), empty], 0)
    pivot_now = pivot_blocks
    identity = jnp.eye(full_width, dtype=jnp.float32)
    saved = []
    for tier_index in range(LEVELS):
        spacing = 2 ** tier_index
        factor = jnp.linalg.cholesky(pivot_now)
        left_solved = solve_batch(factor, lower_now)
        right_solved = solve_batch(factor, upper_now)
        inverse = solve_batch(factor, jnp.broadcast_to(identity, factor.shape))
        drop_left = batch_product(flipped(lower_now), left_solved)
        upper_new = -batch_product(flipped(left_solved), upper_now)
        drop_right = batch_product(flipped(upper_now), right_solved)
        lower_new = -batch_product(flipped(right_solved), lower_now)
        pivot_now = pivot_now - from_above(drop_left, spacing) - from_below(drop_right, spacing)
        upper_now = from_above(upper_new, spacing)
        lower_now = from_below(lower_new, spacing)
        saved.append((left_solved, right_solved, flipped(inverse)))
    reduced_pivot = pivot_now
    diagonal_now = top_diagonal
    next_now = jnp.where((indices + 2 ** LEVELS >= parts_count)[:, None, None], jnp.float32(0.0), top_coupling)
    for tier_index in reversed(range(LEVELS)):
        spacing = 2 ** tier_index
        left_solved, right_solved, inverse_now = saved[tier_index]
        near_diagonal = from_below(diagonal_now, spacing)
        near_next = from_below(next_now, spacing)
        far_diagonal = from_above(diagonal_now, spacing)
        cross_near = batch_product(left_solved, near_diagonal) + batch_product(right_solved, flipped(near_next))
        cross_far = batch_product(left_solved, near_next) + batch_product(right_solved, far_diagonal)
        diagonal_now = inverse_now + batch_product(cross_near, flipped(left_solved)) + batch_product(cross_far, flipped(right_solved))
        next_now = -cross_far
    next_now = jnp.where((indices == parts_count - 1)[:, None, None], jnp.float32(0.0), next_now)
    return (diagonal_now, next_now, reduced_pivot)
```

```python
import functools

import jax
import jax.numpy as jnp
from jax import lax
from jax.experimental import pallas as pl
from jax.experimental.pallas import tpu as pltpu
from jax.sharding import PartitionSpec as P

f32 = jnp.float32
bf16 = jnp.bfloat16
MESH = pl.DeviceIdType.MESH
VMEM = pl.BlockSpec(memory_space=pltpu.VMEM)
LIMIT = 56 * 2**20


def dot(a, b, flip=False, precision=None):
    dims = (((1,), (1 if flip else 0,)), ((), ()))
    return lax.dot_general(a, b, dims, precision=precision, preferred_element_type=f32)


def split(x):
    high = x.astype(bf16)
    return high, (x - high.astype(f32)).astype(bf16)


def dot3(a, b, flip=False):
    ah, al = split(a)
    bh, bl = split(b)
    return dot(ah, bh, flip) + (dot(ah, bl, flip) + dot(al, bh, flip))


def dot1(a, b):
    return dot(a.astype(bf16), b.astype(bf16))


def full_dot(a, b):
    return dot(a, b, precision=lax.Precision.HIGHEST)


def eye(size):
    rows = lax.broadcasted_iota(jnp.int32, (size, size), 0)
    columns = lax.broadcasted_iota(jnp.int32, (size, size), 1)
    return rows == columns


def scales(pivot):
    only = jnp.where(eye(pivot.shape[0]), pivot, 0.0)
    return (
        lax.rsqrt(jnp.sum(only, axis=1, keepdims=True)),
        lax.rsqrt(jnp.sum(only, axis=0, keepdims=True)),
    )


def row_norm(x):
    return jnp.max(jnp.sum(jnp.abs(x), axis=1, keepdims=True), axis=0, keepdims=True)


def newton_start(pivot, x_ref, steps):
    column, row = scales(pivot)
    scaled = pivot * column * row
    factor = jnp.minimum(1.0, 1.9 / row_norm(scaled))
    one = jnp.where(eye(pivot.shape[0]), 1.0, 0.0)
    rest = one - factor * scaled
    x = factor * (one + rest)
    for _ in range(steps):
        rest = dot1(rest, rest)
        x = x + dot1(x, rest)
    x_ref[...] = x


def finish_kernel(pivot_ref, x_ref, out_ref, a_ref):
    size = pivot_ref.shape[0]
    column, row = scales(pivot_ref[...])
    a_ref[...] = pivot_ref[...] * column * row

    def one():
        return jnp.where(eye(size), 1.0, 0.0)

    x = x_ref[...]
    rest = one() - dot3(a_ref[...], x)
    first = row_norm(rest)[0, 0]
    out_ref[...] = x + dot1(x, rest)

    @pl.when(jnp.logical_not(first < 2.0**-7))
    def _():
        @pl.when(jnp.logical_not(first < 0.5))
        def _():
            out_ref[...] = one() / row_norm(a_ref[...])

        def more(state):
            count, norm = state
            return jnp.logical_and(count < 60, jnp.logical_not(norm < 1e-3))

        def step(state):
            count, _ = state
            rest = one() - full_dot(a_ref[...], out_ref[...])
            out_ref[...] = out_ref[...] + full_dot(out_ref[...], rest)
            return count + 1, row_norm(rest)[0, 0]

        lax.while_loop(more, step, (0, jnp.float32(1.0)))

    out_ref[...] = out_ref[...] * column * row


def finish(pivot, x):
    size = pivot.shape[0]
    return pl.pallas_call(
        finish_kernel,
        out_shape=jax.ShapeDtypeStruct((size, size), f32),
        in_specs=[VMEM] * 2,
        out_specs=VMEM,
        scratch_shapes=[pltpu.VMEM((size, size), f32)],
        compiler_params=pltpu.CompilerParams(vmem_limit_bytes=LIMIT),
    )(pivot, x)


class Sender:
    def __init__(self, parts, send_sems, recv_sems):
        self.parts, self.send_sems, self.recv_sems = parts, send_sems, recv_sems
        self.count = 0
        self.part = lax.axis_index("tm")
        self.row = lax.axis_index("rows")
        self.copies = []

    def device(self, parts=0, rows=0):
        return (
            lax.rem(self.part + (parts + self.parts), self.parts),
            lax.rem(self.row + (rows + 4), 4),
        )

    def greet(self, *offsets):
        barrier = pltpu.get_barrier_semaphore()
        for parts, rows in offsets:
            pl.semaphore_signal(barrier, inc=1, device_id=self.device(parts, rows), device_id_type=MESH)
        pl.semaphore_wait(barrier, len(offsets))

    def send(self, source, target, parts=0, rows=0):
        copy = pltpu.make_async_remote_copy(
            src_ref=source,
            dst_ref=target,
            send_sem=self.send_sems.at[self.count],
            recv_sem=self.recv_sems.at[self.count],
            device_id=self.device(parts, rows),
            device_id_type=MESH,
        )
        self.count += 1
        copy.start()
        self.copies.append(copy)
        return copy

    def sent(self):
        for copy in self.copies:
            copy.wait_send()


class Ring:
    def __init__(self, sender, view):
        self.sender, self.view = sender, view
        row = sender.row
        self.left = lax.rem(row + 3, 4)
        self.right = lax.rem(row + 1, 4)
        self.far = lax.rem(row + 2, 4)
        self.first = sender.send(view(row), view(row), rows=1)
        self.second = sender.send(view(row), view(row), rows=-1)

    def forward(self):
        self.first.wait_recv()
        self.third = self.sender.send(self.view(self.left, 0), self.view(self.left, 0), rows=1)
        self.second.wait_recv()
        self.fourth = self.sender.send(self.view(self.right, 1), self.view(self.right, 1), rows=-1)

    def done(self):
        self.third.wait_recv()
        self.fourth.wait_recv()


def columns_of(ref):
    quarter = ref.shape[1] // 4
    half = ref.shape[0] // 2

    def view(q, h=None):
        rows = slice(None) if h is None else pl.ds(h * half, half)
        return ref.at[rows, pl.ds(pl.multiple_of(q * quarter, quarter), quarter)]

    return view


def rows_of(ref):
    quarter = ref.shape[0] // 4
    half = quarter // 2

    def view(q, h=None):
        if h is None:
            return ref.at[pl.ds(pl.multiple_of(q * quarter, quarter), quarter), :]
        return ref.at[pl.ds(pl.multiple_of(q * quarter + h * half, half), half), :]

    return view


def first_kernel(
    parts, pivot_ref, lower_ref, s_ref, w_ref,
    v_ref, next_ref, x_ref, sd_ref, wd_ref, su_ref,
    w_masked, send_sems, recv_sems,
):
    sender = Sender(parts, send_sems, recv_sems)
    part, row = sender.part, sender.row
    quarter = lower_ref.shape[1]
    own = pl.ds(pl.multiple_of(row * quarter, quarter), quarter)
    v_ref[:, own] = jnp.where(part == 0, 0.0, lower_ref[...])
    w_masked[...] = jnp.where(part + 4 >= parts, 0.0, w_ref[...])
    sender.greet((0, 1), (0, -1), (1, 0), (-1, 0), (2, 0), (-2, 0))
    view, target = columns_of(v_ref), columns_of(next_ref)
    ring = Ring(sender, view)
    arriving = [sender.send(view(row), target(row), parts=-1)]
    arriving.append(sender.send(w_masked, wd_ref, parts=2))
    arriving.append(sender.send(s_ref, sd_ref, parts=2))

    newton_start(pivot_ref[...], x_ref, 2)

    ring.forward()
    arriving.append(sender.send(view(ring.left), target(ring.left), parts=-1))
    arriving.append(sender.send(view(ring.right), target(ring.right), parts=-1))
    arriving.append(sender.send(s_ref, su_ref, parts=-2))
    ring.third.wait_recv()
    arriving.append(sender.send(view(ring.far, 0), target(ring.far, 0), parts=-1))
    ring.fourth.wait_recv()
    arriving.append(sender.send(view(ring.far, 1), target(ring.far, 1), parts=-1))
    for copy in arriving:
        copy.wait_recv()
    sender.sent()


def second_kernel(
    parts, pivot_ref, g_ref, v_ref, next_ref, sdq_ref, wdq_ref, suq_ref,
    d2_ref, x_ref, v2_ref, u2_ref, left_ref, right_ref, above_left, above_right, below_right,
    sd_ref, wd_ref, su_ref,
    g_below, g_above, v_below, v_above, z_ref, y_ref, send_sems, recv_sems,
):
    sender = Sender(parts, send_sems, recv_sems)
    row = sender.row
    quarter = suq_ref.shape[0]
    own = pl.ds(pl.multiple_of(row * quarter, quarter), quarter)
    sender.greet((0, 1), (0, -1), (1, 0), (-1, 0))
    from_below = sender.send(g_ref, g_below, parts=1)
    from_above = sender.send(g_ref, g_above, parts=-1)
    wd_ref[own, :] = wdq_ref[...]
    sd_ref[own, :] = sdq_ref[...]
    su_ref[own, :] = suq_ref[...]
    ring_w = Ring(sender, rows_of(wd_ref))
    ring_d = Ring(sender, rows_of(sd_ref))
    ring_u = Ring(sender, rows_of(su_ref))
    v_from_below = sender.send(v_ref, v_below, parts=1)
    v_from_above = sender.send(next_ref, v_above, parts=-1)

    left_ref[...] = dot3(g_ref[...], v_ref[...])
    right_ref[...] = dot3(g_ref[...], next_ref[...], flip=True)

    from_below.wait_recv()
    y_ref[...] = dot3(v_ref[...], g_below[...])
    d2_ref[...] = pivot_ref[...] - dot3(y_ref[...], v_ref[...], flip=True)
    ring_w.forward()
    from_above.wait_recv()
    z_ref[...] = dot3(next_ref[...].T, g_above[...])
    d2_ref[...] = d2_ref[...] - dot3(z_ref[...], next_ref[...])
    ring_d.forward()

    newton_start(d2_ref[...], x_ref, 3)
    ring_u.forward()

    v_from_below.wait_recv()
    v2_ref[...] = -dot3(y_ref[...], v_below[...])
    v_from_above.wait_recv()
    u2_ref[...] = -dot3(z_ref[...], v_above[...], flip=True)
    above_left[...] = dot3(g_above[own, :], next_ref[...])
    above_right[...] = dot3(g_above[own, :], v_above[...], flip=True)
    below_right[...] = dot3(g_below[own, :], v_ref[...], flip=True)
    ring_w.done()
    ring_d.done()
    ring_u.done()
    sender.sent()


def third_kernel(
    parts, d2_ref, g2_ref, v2_ref, u2_ref, g_ref, left_ref, right_ref,
    above_left, above_right, below_right, sd_ref, wd_ref, su_ref,
    s_out, next_out, pivot_out,
    left2, right2, x_ref, y_ref, down_out, up_out, down_in, up_in,
    xs_out, ys_out, yd_out, xs_in, ys_in, yd_in, send_sems, recv_sems,
):
    sender = Sender(parts, send_sems, recv_sems)
    part, row = sender.part, sender.row
    quarter = s_out.shape[0]
    own = pl.ds(pl.multiple_of(row * quarter, quarter), quarter)
    sender.greet((1, 0), (-1, 0), (2, 0), (-2, 0))
    left2[...] = dot3(g2_ref[...], v2_ref[...])
    down_out[...] = dot3(v2_ref[:, own].T, left2[...])
    from_above = sender.send(down_out, down_in, parts=-2)
    right2[...] = dot3(g2_ref[...], u2_ref[...])
    up_out[...] = dot3(u2_ref[:, own].T, right2[...])
    from_below = sender.send(up_out, up_in, parts=2)

    y_ref[...] = dot3(left2[...], wd_ref[...]) + dot3(right2[...], su_ref[...])
    ys_out[...] = -dot3(above_left[...], y_ref[...])
    ys = sender.send(ys_out, ys_in, parts=1)
    x_ref[...] = dot3(left2[...], sd_ref[...]) + dot3(right2[...], wd_ref[...], flip=True)
    x_ref[...] = g2_ref[...] + dot3(x_ref[...], left2[...], flip=True) + dot3(
        y_ref[...], right2[...], flip=True
    )
    xs_out[...] = dot3(above_left[...], x_ref[...]) - dot3(above_right[...], y_ref[...], flip=True)
    xs = sender.send(xs_out, xs_in, parts=1)
    yd_out[...] = dot3(below_right[...], x_ref[...])
    yd = sender.send(yd_out, yd_in, parts=-1)

    from_above.wait_recv()
    from_below.wait_recv()
    pivot_out[...] = d2_ref[own, :] - down_in[...] - up_in[...]
    xs.wait_recv()
    s_out[...] = g_ref[own, :] + dot3(xs_in[...], left_ref[...], flip=True)
    ys.wait_recv()
    yd.wait_recv()
    y = ys_in[...] + yd_in[...]
    s_out[...] = s_out[...] + dot3(y, right_ref[...], flip=True)
    next_out[...] = jnp.where(part == parts - 1, 0.0, -y)
    sender.sent()


def local(pivot_blocks, lower_blocks, top_diagonal, top_coupling):
    parts = lax.axis_size("tm")
    size = pivot_blocks.shape[1]
    quarter = lower_blocks.shape[2]
    whole = jax.ShapeDtypeStruct((size, size), f32)
    strip = jax.ShapeDtypeStruct((quarter, size), f32)
    whole_space = pltpu.VMEM((size, size), f32)
    strip_space = pltpu.VMEM((quarter, size), f32)

    def call(kernel, identity, operands, results, scratch, copies):
        return pl.pallas_call(
            functools.partial(kernel, parts),
            out_shape=tuple(results),
            in_specs=[VMEM] * len(operands),
            out_specs=(VMEM,) * len(results),
            scratch_shapes=list(scratch)
            + [pltpu.SemaphoreType.DMA((copies,)), pltpu.SemaphoreType.DMA((copies,))],
            compiler_params=pltpu.CompilerParams(
                collective_id=identity, has_side_effects=True, vmem_limit_bytes=LIMIT
            ),
        )(*operands)

    pivot = pivot_blocks[0]
    v, v_next, x, sdq, wdq, suq = call(
        first_kernel, 0,
        (pivot, lower_blocks[0], top_diagonal[0], top_coupling[0]),
        [whole, whole, whole, strip, strip, strip], [strip_space], 12,
    )
    g = finish(pivot, x)
    d2, x2, v2, u2, left, right, above_left, above_right, below_right, sd, wd, su = call(
        second_kernel, 1,
        (pivot, g, v, v_next, sdq, wdq, suq),
        [whole] * 6 + [strip] * 3 + [whole] * 3, [whole_space] * 6, 16,
    )
    g2 = finish(d2, x2)
    s, coupling, reduced = call(
        third_kernel, 2,
        (d2, g2, v2, u2, g, left, right, above_left, above_right, below_right, sd, wd, su),
        [strip] * 3, [whole_space] * 4 + [strip_space] * 10, 5,
    )
    return (s[None], coupling[None], reduced[None])


def solution(mesh):
    placed = (
        P("tm", None, None),
        P("tm", None, "rows"),
        P("tm", "rows", None),
        P("tm", "rows", None),
    )
    return jax.shard_map(
        local,
        mesh=mesh,
        in_specs=placed,
        out_specs=(P("tm", "rows", None), P("tm", "rows", None), P("tm", "rows", None)),
        check_vma=False,
    )
```

```python
import functools

import jax
import jax.numpy as jnp
from jax import lax
from jax.experimental import pallas as pl
from jax.experimental.pallas import tpu as pltpu
from jax.sharding import PartitionSpec as P

f32 = jnp.float32
bf16 = jnp.bfloat16
MESH = pl.DeviceIdType.MESH
VMEM = pl.BlockSpec(memory_space=pltpu.VMEM)
LIMIT = 36 * 2**20


def dot(a, b, flip=False, precision=None):
    dims = (((1,), (1 if flip else 0,)), ((), ()))
    return lax.dot_general(a, b, dims, precision=precision, preferred_element_type=f32)


def split(x):
    high = x.astype(bf16)
    return high, (x - high.astype(f32)).astype(bf16)


def dot3(a, b, flip=False):
    ah, al = split(a)
    bh, bl = split(b)
    return dot(ah, bh, flip) + (dot(ah, bl, flip) + dot(al, bh, flip))


def dot1(a, b):
    return dot(a.astype(bf16), b.astype(bf16))


def full_dot(a, b):
    return dot(a, b, precision=lax.Precision.HIGHEST)


def eye(size):
    rows = lax.broadcasted_iota(jnp.int32, (size, size), 0)
    columns = lax.broadcasted_iota(jnp.int32, (size, size), 1)
    return rows == columns


def scales(pivot):
    only = jnp.where(eye(pivot.shape[0]), pivot, 0.0)
    return (
        lax.rsqrt(jnp.sum(only, axis=1, keepdims=True)),
        lax.rsqrt(jnp.sum(only, axis=0, keepdims=True)),
    )


def row_norm(x):
    return jnp.max(jnp.sum(jnp.abs(x), axis=1, keepdims=True), axis=0, keepdims=True)


def newton_start(scaled, steps):
    factor = jnp.minimum(1.0, 1.9 / row_norm(scaled))
    one = jnp.where(eye(scaled.shape[0]), 1.0, 0.0)
    rest = one - factor * scaled
    x = factor * (one + rest)
    for _ in range(steps):
        rest = dot1(rest, rest)
        x = x + dot1(x, rest)
    return x


def newton_end(x, out_ref, a_ref):
    size = a_ref.shape[0]

    def one():
        return jnp.where(eye(size), 1.0, 0.0)

    rest = one() - dot3(a_ref[...], x)
    first = row_norm(rest)[0, 0]
    out_ref[...] = x + dot1(x, rest)

    @pl.when(jnp.logical_not(first < 2.0**-7))
    def _():
        @pl.when(jnp.logical_not(first < 0.5))
        def _():
            out_ref[...] = one() / row_norm(a_ref[...])

        def more(state):
            count, norm = state
            return jnp.logical_and(count < 60, jnp.logical_not(norm < 1e-3))

        def step(state):
            count, _ = state
            rest = one() - full_dot(a_ref[...], out_ref[...])
            out_ref[...] = out_ref[...] + full_dot(out_ref[...], rest)
            return count + 1, row_norm(rest)[0, 0]

        lax.while_loop(more, step, (0, jnp.float32(1.0)))


def inverse_kernel(pivot_ref, out_ref, a_ref):
    column, row = scales(pivot_ref[...])
    a_ref[...] = pivot_ref[...] * column * row
    newton_end(newton_start(a_ref[...], 2), out_ref, a_ref)
    out_ref[...] = out_ref[...] * column * row


def finish_kernel(pivot_ref, x_ref, out_ref, a_ref):
    column, row = scales(pivot_ref[...])
    a_ref[...] = pivot_ref[...] * column * row
    newton_end(x_ref[...], out_ref, a_ref)
    out_ref[...] = out_ref[...] * column * row


def inverse(kernel, *operands):
    size = operands[0].shape[0]
    return pl.pallas_call(
        kernel,
        out_shape=jax.ShapeDtypeStruct((size, size), f32),
        in_specs=[VMEM] * len(operands),
        out_specs=VMEM,
        scratch_shapes=[pltpu.VMEM((size, size), f32)],
        compiler_params=pltpu.CompilerParams(vmem_limit_bytes=LIMIT),
    )(*operands)


class Sender:
    def __init__(self, parts, send_sems, recv_sems):
        self.parts, self.send_sems, self.recv_sems = parts, send_sems, recv_sems
        self.count = 0
        self.part = lax.axis_index("tm")
        self.row = lax.axis_index("rows")
        self.copies = []

    def device(self, parts=0, rows=0):
        return (
            lax.rem(self.part + (parts + self.parts), self.parts),
            lax.rem(self.row + (rows + 4), 4),
        )

    def greet(self, *offsets):
        barrier = pltpu.get_barrier_semaphore()
        for parts, rows in offsets:
            pl.semaphore_signal(barrier, inc=1, device_id=self.device(parts, rows), device_id_type=MESH)
        pl.semaphore_wait(barrier, len(offsets))

    def plan(self, source, target, parts=0, rows=0):
        copy = pltpu.make_async_remote_copy(
            src_ref=source,
            dst_ref=target,
            send_sem=self.send_sems.at[self.count],
            recv_sem=self.recv_sems.at[self.count],
            device_id=self.device(parts, rows),
            device_id_type=MESH,
        )
        self.count += 1
        return copy

    def send(self, source, target, parts=0, rows=0):
        copy = self.plan(source, target, parts, rows)
        copy.start()
        self.copies.append(copy)
        return copy

    def sent(self):
        for copy in self.copies:
            copy.wait_send()


class Ring:
    def __init__(self, sender, view):
        row = sender.row
        left, right = lax.rem(row + 3, 4), lax.rem(row + 1, 4)
        self.first = sender.plan(view(row), view(row), rows=1)
        self.second = sender.plan(view(row), view(row), rows=-1)
        self.third = sender.plan(view(left, 0), view(left, 0), rows=1)
        self.fourth = sender.plan(view(right, 1), view(right, 1), rows=-1)

    def start(self):
        self.first.start()
        self.second.start()

    def forward(self):
        self.first.wait_recv()
        self.third.start()
        self.second.wait_recv()
        self.fourth.start()

    def done(self):
        self.third.wait_recv()
        self.fourth.wait_recv()

    def sent(self):
        for copy in (self.first, self.second, self.third, self.fourth):
            copy.wait_send()


def upper(ref, i):
    step = ref.shape[0] // 4
    return ref.at[pl.ds(i * step, step), pl.ds(i * step, (4 - i) * step)]


def mirror(ref):
    step = ref.shape[0] // 4
    for i in range(4):
        for j in range(i + 1, 4):
            here, there = pl.ds(i * step, step), pl.ds(j * step, step)
            ref[there, here] = ref[here, there].T


def columns_of(ref):
    quarter = ref.shape[1] // 4
    half = ref.shape[0] // 2

    def view(q, h=None):
        rows = slice(None) if h is None else pl.ds(h * half, half)
        return ref.at[rows, pl.ds(pl.multiple_of(q * quarter, quarter), quarter)]

    return view


def rows_of(ref):
    quarter = ref.shape[0] // 4
    half = quarter // 2

    def view(q, h=None):
        if h is None:
            return ref.at[pl.ds(pl.multiple_of(q * quarter, quarter), quarter), :]
        return ref.at[pl.ds(pl.multiple_of(q * quarter + h * half, half), half), :]

    return view


def second_kernel(
    parts, pivot_ref, lower_ref, s_ref, w_ref, g_ref,
    d2_ref, x_ref, v2_ref, u2_ref, left_ref, right_ref, above_left, above_right, below_right,
    wd_ref, su_ref, sdq_ref,
    v_ref, next_ref, w_masked, g_below, g_above, v_below, v_above, z_ref, y_ref,
    send_sems, recv_sems,
):
    sender = Sender(parts, send_sems, recv_sems)
    part, row = sender.part, sender.row
    odd = lax.rem(part, 2) == 1
    even = lax.rem(part, 2) == 0
    quarter = lower_ref.shape[1]
    own = pl.ds(pl.multiple_of(row * quarter, quarter), quarter)
    left, right, far = (lax.rem(row + i, 4) for i in (3, 1, 2))
    v_ref[:, own] = jnp.where(part == 0, 0.0, lower_ref[...])
    w_masked[...] = jnp.where(part + 4 >= parts, 0.0, w_ref[...])
    view, target = columns_of(v_ref), columns_of(next_ref)
    sender.greet((0, 1), (0, -1), (1, 0), (-1, 0), (2, 0), (-2, 0))

    next_own = sender.send(view(row), target(row), parts=-1)
    ring_v = Ring(sender, view)
    ring_v.start()
    w_own = sender.send(w_masked, rows_of(wd_ref)(row), parts=2)
    from_below = [sender.send(upper(g_ref, i), upper(g_below, i), parts=1) for i in range(4)]
    from_above = [sender.send(upper(g_ref, i), upper(g_above, i), parts=-1) for i in range(4)]
    su_own = sender.send(s_ref, rows_of(su_ref)(row), parts=-2)
    ring_next = Ring(sender, target)
    passed = [
        sender.plan(view(q, h), target(q, h), parts=-1)
        for q, h in ((left, None), (right, None), (far, 0), (far, 1))
    ]

    next_own.wait_recv()

    @pl.when(odd)
    def _():
        ring_next.start()

    ring_v.forward()

    @pl.when(odd)
    def _():
        passed[0].start()
        passed[1].start()

    w_own.wait_recv()
    ring_w = Ring(sender, rows_of(wd_ref))
    ring_w.start()

    @pl.when(odd)
    def _():
        ring_next.forward()

    ring_v.done()

    @pl.when(odd)
    def _():
        passed[2].start()
        passed[3].start()

    v_from_below = sender.send(v_ref, v_below, parts=1)
    sd_own = sender.send(s_ref, sdq_ref, parts=2)
    left_ref[...] = dot3(g_ref[...], v_ref[...])

    @pl.when(odd)
    def _():
        ring_next.done()

    @pl.when(even)
    def _():
        for copy in passed:
            copy.wait_recv()

    v_from_above = sender.send(next_ref, v_above, parts=-1)

    for copy in from_below:
        copy.wait_recv()
    mirror(g_below)
    y_ref[...] = dot3(v_ref[...], g_below[...])
    d2_ref[...] = pivot_ref[...] - dot3(y_ref[...], v_ref[...], flip=True)
    su_own.wait_recv()
    ring_u = Ring(sender, rows_of(su_ref))
    ring_u.start()
    for copy in from_above:
        copy.wait_recv()
    mirror(g_above)
    z_ref[...] = dot3(next_ref[...].T, g_above[...])
    d2_ref[...] = d2_ref[...] - dot3(z_ref[...], next_ref[...])
    ring_w.forward()

    column, line = scales(d2_ref[...])
    x_ref[...] = newton_start(d2_ref[...] * column * line, 3)
    right_ref[...] = dot3(g_ref[...], next_ref[...], flip=True)
    above_left[...] = dot3(g_above[own, :], next_ref[...])
    below_right[...] = dot3(g_below[own, :], v_ref[...], flip=True)
    ring_u.forward()

    v_from_above.wait_recv()
    u2_ref[...] = -dot3(z_ref[...], v_above[...], flip=True)
    above_right[...] = dot3(g_above[own, :], v_above[...], flip=True)
    v_from_below.wait_recv()
    v2_ref[...] = -dot3(y_ref[...], v_below[...])
    sd_own.wait_recv()
    ring_w.done()
    ring_u.done()
    sender.sent()
    for ring in (ring_v, ring_w, ring_u):
        ring.sent()

    @pl.when(odd)
    def _():
        ring_next.sent()
        for copy in passed:
            copy.wait_send()


def third_kernel(
    parts, g2_ref, v2_ref, u2_ref, left_ref, right_ref,
    above_left, above_right, below_right, wd_ref, su_ref, sdq_ref,
    s_out, y_out, down_in, up_in,
    sd_ref, left2, right2, x_ref, y_ref, down_out, up_out,
    xs_out, ys_out, yd_out, xs_in, ys_in, yd_in, send_sems, recv_sems,
):
    sender = Sender(parts, send_sems, recv_sems)
    row = sender.row
    quarter = s_out.shape[0]
    own = pl.ds(pl.multiple_of(row * quarter, quarter), quarter)
    sd_ref[own, :] = sdq_ref[...]
    sender.greet((0, 1), (0, -1), (1, 0), (-1, 0), (2, 0), (-2, 0))
    ring_d = Ring(sender, rows_of(sd_ref))
    ring_d.start()
    left2[...] = dot3(g2_ref[...], v2_ref[...])
    right2[...] = dot3(g2_ref[...], u2_ref[...])
    y_ref[...] = dot3(left2[...], wd_ref[...]) + dot3(right2[...], su_ref[...])
    ys_out[...] = -dot3(above_left[...], y_ref[...])
    ys = sender.send(ys_out, ys_in, parts=1)
    ring_d.forward()
    down_out[...] = dot3(v2_ref[:, own].T, left2[...])
    from_above = sender.send(down_out, down_in, parts=-2)
    up_out[...] = dot3(u2_ref[:, own].T, right2[...])
    from_below = sender.send(up_out, up_in, parts=2)
    x_ref[...] = dot3(right2[...], wd_ref[...], flip=True)
    ring_d.done()
    x_ref[...] = x_ref[...] + dot3(left2[...], sd_ref[...])
    x_ref[...] = g2_ref[...] + dot3(x_ref[...], left2[...], flip=True) + dot3(
        y_ref[...], right2[...], flip=True
    )
    xs_out[...] = dot3(above_left[...], x_ref[...]) - dot3(above_right[...], y_ref[...], flip=True)
    xs = sender.send(xs_out, xs_in, parts=1)
    yd_out[...] = dot3(below_right[...], x_ref[...])
    yd = sender.send(yd_out, yd_in, parts=-1)

    from_above.wait_recv()
    from_below.wait_recv()
    ys.wait_recv()
    yd.wait_recv()
    y_out[...] = ys_in[...] + yd_in[...]
    s_out[...] = dot3(y_out[...], right_ref[...], flip=True)
    xs.wait_recv()
    s_out[...] = s_out[...] + dot3(xs_in[...], left_ref[...], flip=True)
    sender.sent()
    ring_d.sent()


def local(pivot_blocks, lower_blocks, top_diagonal, top_coupling):
    parts = lax.axis_size("tm")
    size = pivot_blocks.shape[1]
    quarter = lower_blocks.shape[2]
    whole = jax.ShapeDtypeStruct((size, size), f32)
    strip = jax.ShapeDtypeStruct((quarter, size), f32)
    whole_space = pltpu.VMEM((size, size), f32)
    strip_space = pltpu.VMEM((quarter, size), f32)

    def call(kernel, identity, operands, results, scratch, copies):
        return pl.pallas_call(
            functools.partial(kernel, parts),
            out_shape=tuple(results),
            in_specs=[VMEM] * len(operands),
            out_specs=(VMEM,) * len(results),
            scratch_shapes=list(scratch)
            + [pltpu.SemaphoreType.DMA((copies,)), pltpu.SemaphoreType.DMA((copies,))],
            compiler_params=pltpu.CompilerParams(
                collective_id=identity, has_side_effects=True, vmem_limit_bytes=LIMIT
            ),
        )(*operands)

    pivot = pivot_blocks[0]
    g = inverse(inverse_kernel, pivot)
    d2, x2, v2, u2, left, right, above_left, above_right, below_right, wd, su, sdq = call(
        second_kernel, 0,
        (pivot, lower_blocks[0], top_diagonal[0], top_coupling[0], g),
        [whole] * 6 + [strip] * 3 + [whole] * 2 + [strip],
        [whole_space] * 2 + [strip_space] + [whole_space] * 6, 34,
    )
    g2 = inverse(finish_kernel, d2, x2)
    s, y, down, up = call(
        third_kernel, 1,
        (g2, v2, u2, left, right, above_left, above_right, below_right, wd, su, sdq),
        [strip] * 4, [whole_space] * 5 + [strip_space] * 8, 9,
    )
    start = lax.axis_index("rows") * quarter
    s = lax.dynamic_slice_in_dim(g, start, quarter, 0) + s
    reduced = lax.dynamic_slice_in_dim(d2, start, quarter, 0) - down - up
    coupling = jnp.where(lax.axis_index("tm") == parts - 1, 0.0, -y)
    return (s[None], coupling[None], reduced[None])


def solution(mesh):
    placed = (
        P("tm", None, None),
        P("tm", None, "rows"),
        P("tm", "rows", None),
        P("tm", "rows", None),
    )
    return jax.shard_map(
        local,
        mesh=mesh,
        in_specs=placed,
        out_specs=(P("tm", "rows", None), P("tm", "rows", None), P("tm", "rows", None)),
        check_vma=False,
    )
```

```python
import functools

import jax
import jax.numpy as jnp
from jax import lax
from jax.experimental import pallas as pl
from jax.experimental.pallas import tpu as pltpu
from jax.sharding import PartitionSpec as P

f32 = jnp.float32
bf16 = jnp.bfloat16
MESH = pl.DeviceIdType.MESH
VMEM = pl.BlockSpec(memory_space=pltpu.VMEM)
LIMIT = 36 * 2**20


def dot(a, b, flip=False, precision=None):
    dims = (((1,), (1 if flip else 0,)), ((), ()))
    return lax.dot_general(a, b, dims, precision=precision, preferred_element_type=f32)


def split(x):
    high = x.astype(bf16)
    return high, (x - high.astype(f32)).astype(bf16)


def dot3(a, b, flip=False):
    ah, al = split(a)
    bh, bl = split(b)
    return dot(ah, bh, flip) + (dot(ah, bl, flip) + dot(al, bh, flip))


def dot1(a, b):
    return dot(a.astype(bf16), b.astype(bf16))


def full_dot(a, b):
    return dot(a, b, precision=lax.Precision.HIGHEST)


def eye(size):
    rows = lax.broadcasted_iota(jnp.int32, (size, size), 0)
    columns = lax.broadcasted_iota(jnp.int32, (size, size), 1)
    return rows == columns


def scales(pivot):
    only = jnp.where(eye(pivot.shape[0]), pivot, 0.0)
    return (
        lax.rsqrt(jnp.sum(only, axis=1, keepdims=True)),
        lax.rsqrt(jnp.sum(only, axis=0, keepdims=True)),
    )


def row_norm(x):
    return jnp.max(jnp.sum(jnp.abs(x), axis=1, keepdims=True), axis=0, keepdims=True)


def newton_start(scaled, steps):
    factor = jnp.minimum(1.0, 1.9 / row_norm(scaled))
    one = jnp.where(eye(scaled.shape[0]), 1.0, 0.0)
    rest = one - factor * scaled
    x = factor * (one + rest)
    for _ in range(steps):
        rest = dot1(rest, rest)
        x = x + dot1(x, rest)
    return x


def newton_end(x, out_ref, a_ref):
    size = a_ref.shape[0]

    def one():
        return jnp.where(eye(size), 1.0, 0.0)

    rest = one() - dot3(a_ref[...], x)
    first = row_norm(rest)[0, 0]
    out_ref[...] = x + dot1(x, rest)

    @pl.when(jnp.logical_not(first < 2.0**-7))
    def _():
        @pl.when(jnp.logical_not(first < 0.5))
        def _():
            out_ref[...] = one() / row_norm(a_ref[...])

        def more(state):
            count, norm = state
            return jnp.logical_and(count < 60, jnp.logical_not(norm < 1e-3))

        def step(state):
            count, _ = state
            rest = one() - full_dot(a_ref[...], out_ref[...])
            out_ref[...] = out_ref[...] + full_dot(out_ref[...], rest)
            return count + 1, row_norm(rest)[0, 0]

        lax.while_loop(more, step, (0, jnp.float32(1.0)))


def inverse_kernel(pivot_ref, out_ref, a_ref):
    column, row = scales(pivot_ref[...])
    a_ref[...] = pivot_ref[...] * column * row
    newton_end(newton_start(a_ref[...], 2), out_ref, a_ref)
    out_ref[...] = out_ref[...] * column * row


def finish_kernel(pivot_ref, x_ref, out_ref, a_ref):
    column, row = scales(pivot_ref[...])
    a_ref[...] = pivot_ref[...] * column * row
    newton_end(x_ref[...], out_ref, a_ref)
    out_ref[...] = out_ref[...] * column * row


def inverse(kernel, *operands):
    size = operands[0].shape[0]
    return pl.pallas_call(
        kernel,
        out_shape=jax.ShapeDtypeStruct((size, size), f32),
        in_specs=[VMEM] * len(operands),
        out_specs=VMEM,
        scratch_shapes=[pltpu.VMEM((size, size), f32)],
        compiler_params=pltpu.CompilerParams(vmem_limit_bytes=LIMIT),
    )(*operands)


class Sender:
    def __init__(self, parts, send_sems, recv_sems):
        self.parts, self.send_sems, self.recv_sems = parts, send_sems, recv_sems
        self.count = 0
        self.part = lax.axis_index("tm")
        self.row = lax.axis_index("rows")
        self.copies = []

    def device(self, parts=0, rows=0):
        return (
            lax.rem(self.part + (parts + self.parts), self.parts),
            lax.rem(self.row + (rows + 4), 4),
        )

    def greet(self, *offsets):
        barrier = pltpu.get_barrier_semaphore()
        for parts, rows in offsets:
            pl.semaphore_signal(barrier, inc=1, device_id=self.device(parts, rows), device_id_type=MESH)
        pl.semaphore_wait(barrier, len(offsets))

    def plan(self, source, target, parts=0, rows=0):
        copy = pltpu.make_async_remote_copy(
            src_ref=source,
            dst_ref=target,
            send_sem=self.send_sems.at[self.count],
            recv_sem=self.recv_sems.at[self.count],
            device_id=self.device(parts, rows),
            device_id_type=MESH,
        )
        self.count += 1
        return copy

    def send(self, source, target, parts=0, rows=0):
        copy = self.plan(source, target, parts, rows)
        copy.start()
        self.copies.append(copy)
        return copy

    def sent(self):
        for copy in self.copies:
            copy.wait_send()


class Ring:
    def __init__(self, sender, view):
        row = sender.row
        left, right = lax.rem(row + 3, 4), lax.rem(row + 1, 4)
        self.first = sender.plan(view(row), view(row), rows=1)
        self.second = sender.plan(view(row), view(row), rows=-1)
        self.third = sender.plan(view(left, 0), view(left, 0), rows=1)
        self.fourth = sender.plan(view(right, 1), view(right, 1), rows=-1)

    def start(self):
        self.first.start()
        self.second.start()

    def forward(self):
        self.first.wait_recv()
        self.third.start()
        self.second.wait_recv()
        self.fourth.start()

    def done(self):
        self.third.wait_recv()
        self.fourth.wait_recv()

    def sent(self):
        for copy in (self.first, self.second, self.third, self.fourth):
            copy.wait_send()


def upper(ref, i):
    step = ref.shape[0] // 4
    return ref.at[pl.ds(i * step, step), pl.ds(i * step, (4 - i) * step)]


def mirror(ref):
    step = ref.shape[0] // 4
    for i in range(4):
        for j in range(i + 1, 4):
            here, there = pl.ds(i * step, step), pl.ds(j * step, step)
            ref[there, here] = ref[here, there].T


def columns_of(ref):
    quarter = ref.shape[1] // 4
    half = ref.shape[0] // 2

    def view(q, h=None):
        rows = slice(None) if h is None else pl.ds(h * half, half)
        return ref.at[rows, pl.ds(pl.multiple_of(q * quarter, quarter), quarter)]

    return view


def rows_of(ref):
    quarter = ref.shape[0] // 4
    half = quarter // 2

    def view(q, h=None):
        if h is None:
            return ref.at[pl.ds(pl.multiple_of(q * quarter, quarter), quarter), :]
        return ref.at[pl.ds(pl.multiple_of(q * quarter + h * half, half), half), :]

    return view


def second_kernel(
    parts, pivot_ref, lower_ref, s_ref, w_ref, g_ref,
    d2_ref, x_ref, v2_ref, u2_ref, left_ref, right_ref, above_left, above_right, below_right,
    wd_ref, su_ref, sdq_ref,
    v_ref, next_ref, w_masked, g_below, g_above, v_below, v_above, z_ref, y_ref,
    send_sems, recv_sems,
):
    sender = Sender(parts, send_sems, recv_sems)
    part, row = sender.part, sender.row
    odd = lax.rem(part, 2) == 1
    even = lax.rem(part, 2) == 0
    quarter = lower_ref.shape[1]
    own = pl.ds(pl.multiple_of(row * quarter, quarter), quarter)
    left, right, far = (lax.rem(row + i, 4) for i in (3, 1, 2))
    v_ref[:, own] = jnp.where(part == 0, 0.0, lower_ref[...])
    w_masked[...] = jnp.where(part + 4 >= parts, 0.0, w_ref[...])
    view, target = columns_of(v_ref), columns_of(next_ref)
    sender.greet((0, 1), (0, -1), (1, 0), (-1, 0), (2, 0), (-2, 0))

    next_own = sender.send(view(row), target(row), parts=-1)
    ring_v = Ring(sender, view)
    ring_v.start()
    w_own = sender.send(w_masked, rows_of(wd_ref)(row), parts=2)
    su_own = sender.send(s_ref, rows_of(su_ref)(row), parts=-2)
    from_below = [sender.send(upper(g_ref, i), upper(g_below, i), parts=1) for i in range(4)]
    from_above = [sender.send(upper(g_ref, i), upper(g_above, i), parts=-1) for i in range(4)]
    ring_next = Ring(sender, target)
    passed = [
        sender.plan(view(q, h), target(q, h), parts=-1)
        for q, h in ((left, None), (right, None), (far, 0), (far, 1))
    ]
    v_from_above = sender.plan(next_ref, v_above, parts=-1)

    next_own.wait_recv()

    @pl.when(odd)
    def _():
        ring_next.start()

    ring_v.forward()

    @pl.when(odd)
    def _():
        passed[0].start()
        passed[1].start()

    w_own.wait_recv()
    ring_w = Ring(sender, rows_of(wd_ref))
    ring_w.start()
    su_own.wait_recv()
    ring_u = Ring(sender, rows_of(su_ref))
    ring_u.start()

    @pl.when(odd)
    def _():
        ring_next.forward()

    ring_v.done()

    @pl.when(odd)
    def _():
        passed[2].start()
        passed[3].start()

    v_from_below = sender.send(v_ref, v_below, parts=1)
    sd_own = sender.send(s_ref, sdq_ref, parts=2)
    left_ref[...] = dot3(g_ref[...], v_ref[...])

    @pl.when(even)
    def _():
        for copy in passed:
            copy.wait_recv()
        v_from_above.start()

    for copy in from_below:
        copy.wait_recv()
    mirror(g_below)
    y_ref[...] = dot3(v_ref[...], g_below[...])
    d2_ref[...] = pivot_ref[...] - dot3(y_ref[...], v_ref[...], flip=True)
    ring_w.forward()
    below_right[...] = dot3(g_below[own, :], v_ref[...], flip=True)

    @pl.when(odd)
    def _():
        ring_next.done()
        v_from_above.start()

    for copy in from_above:
        copy.wait_recv()
    mirror(g_above)
    z_ref[...] = dot3(next_ref[...].T, g_above[...])
    d2_ref[...] = d2_ref[...] - dot3(z_ref[...], next_ref[...])

    column, line = scales(d2_ref[...])
    x_ref[...] = newton_start(d2_ref[...] * column * line, 3)
    ring_u.forward()
    right_ref[...] = dot3(g_ref[...], next_ref[...], flip=True)
    above_left[...] = dot3(g_above[own, :], next_ref[...])
    v_from_below.wait_recv()
    v2_ref[...] = -dot3(y_ref[...], v_below[...])
    v_from_above.wait_recv()
    u2_ref[...] = -dot3(z_ref[...], v_above[...], flip=True)
    above_right[...] = dot3(g_above[own, :], v_above[...], flip=True)
    sd_own.wait_recv()
    ring_w.done()
    ring_u.done()
    sender.sent()
    v_from_above.wait_send()
    for ring in (ring_v, ring_w, ring_u):
        ring.sent()

    @pl.when(odd)
    def _():
        ring_next.sent()
        for copy in passed:
            copy.wait_send()


def third_kernel(
    parts, g2_ref, v2_ref, u2_ref, left_ref, right_ref,
    above_left, above_right, below_right, wd_ref, su_ref, sdq_ref,
    s_out, y_out, down_in, up_in,
    sd_ref, left2, c_ref, x_ref, y_ref, down_out, up_out,
    xs_out, ys_out, yd_out, xs_in, ys_in, yd_in, send_sems, recv_sems,
):
    sender = Sender(parts, send_sems, recv_sems)
    row = sender.row
    quarter = s_out.shape[0]
    own = pl.ds(pl.multiple_of(row * quarter, quarter), quarter)
    sd_ref[own, :] = sdq_ref[...]
    sender.greet((0, 1), (0, -1), (1, 0), (-1, 0), (2, 0), (-2, 0))
    ring_d = Ring(sender, rows_of(sd_ref))
    ring_d.start()
    c_ref[...] = dot3(v2_ref[...], wd_ref[...]) + dot3(u2_ref[...], su_ref[...])
    y_ref[...] = dot3(g2_ref[...], c_ref[...])
    ys_out[...] = -dot3(above_left[...], y_ref[...])
    ys = sender.send(ys_out, ys_in, parts=1)
    left2[...] = dot3(g2_ref[...], v2_ref[...])
    down_out[...] = dot3(v2_ref[:, own].T, left2[...])
    from_above = sender.send(down_out, down_in, parts=-2)
    x_ref[...] = dot3(g2_ref[...], u2_ref[...])
    up_out[...] = dot3(u2_ref[:, own].T, x_ref[...])
    from_below = sender.send(up_out, up_in, parts=2)
    x_ref[...] = dot3(u2_ref[...], wd_ref[...], flip=True)
    ring_d.forward()
    x_ref[...] = dot3(x_ref[...], v2_ref[...], flip=True) + dot3(
        c_ref[...], u2_ref[...], flip=True
    )
    c_ref[...] = dot3(g2_ref[...], x_ref[...])
    x_ref[...] = g2_ref[...] + dot3(c_ref[...], g2_ref[...])
    ring_d.done()
    c_ref[...] = dot3(left2[...], sd_ref[...])
    x_ref[...] = x_ref[...] + dot3(c_ref[...], left2[...], flip=True)
    xs_out[...] = dot3(above_left[...], x_ref[...]) - dot3(above_right[...], y_ref[...], flip=True)
    xs = sender.send(xs_out, xs_in, parts=1)
    yd_out[...] = dot3(below_right[...], x_ref[...])
    yd = sender.send(yd_out, yd_in, parts=-1)

    from_above.wait_recv()
    from_below.wait_recv()
    ys.wait_recv()
    yd.wait_recv()
    y_out[...] = ys_in[...] + yd_in[...]
    s_out[...] = dot3(y_out[...], right_ref[...], flip=True)
    xs.wait_recv()
    s_out[...] = s_out[...] + dot3(xs_in[...], left_ref[...], flip=True)
    sender.sent()
    ring_d.sent()


def local(pivot_blocks, lower_blocks, top_diagonal, top_coupling):
    parts = lax.axis_size("tm")
    size = pivot_blocks.shape[1]
    quarter = lower_blocks.shape[2]
    whole = jax.ShapeDtypeStruct((size, size), f32)
    strip = jax.ShapeDtypeStruct((quarter, size), f32)
    whole_space = pltpu.VMEM((size, size), f32)
    strip_space = pltpu.VMEM((quarter, size), f32)

    def call(kernel, identity, operands, results, scratch, copies):
        return pl.pallas_call(
            functools.partial(kernel, parts),
            out_shape=tuple(results),
            in_specs=[VMEM] * len(operands),
            out_specs=(VMEM,) * len(results),
            scratch_shapes=list(scratch)
            + [pltpu.SemaphoreType.DMA((copies,)), pltpu.SemaphoreType.DMA((copies,))],
            compiler_params=pltpu.CompilerParams(
                collective_id=identity, has_side_effects=True, vmem_limit_bytes=LIMIT
            ),
        )(*operands)

    pivot = pivot_blocks[0]
    g = inverse(inverse_kernel, pivot)
    d2, x2, v2, u2, left, right, above_left, above_right, below_right, wd, su, sdq = call(
        second_kernel, 0,
        (pivot, lower_blocks[0], top_diagonal[0], top_coupling[0], g),
        [whole] * 6 + [strip] * 3 + [whole] * 2 + [strip],
        [whole_space] * 2 + [strip_space] + [whole_space] * 6, 34,
    )
    g2 = inverse(finish_kernel, d2, x2)
    s, y, down, up = call(
        third_kernel, 1,
        (g2, v2, u2, left, right, above_left, above_right, below_right, wd, su, sdq),
        [strip] * 4, [whole_space] * 5 + [strip_space] * 8, 9,
    )
    start = lax.axis_index("rows") * quarter
    s = lax.dynamic_slice_in_dim(g, start, quarter, 0) + s
    reduced = lax.dynamic_slice_in_dim(d2, start, quarter, 0) - down - up
    coupling = jnp.where(lax.axis_index("tm") == parts - 1, 0.0, -y)
    return (s[None], coupling[None], reduced[None])


def solution(mesh):
    placed = (
        P("tm", None, None),
        P("tm", None, "rows"),
        P("tm", "rows", None),
        P("tm", "rows", None),
    )
    return jax.shard_map(
        local,
        mesh=mesh,
        in_specs=placed,
        out_specs=(P("tm", "rows", None), P("tm", "rows", None), P("tm", "rows", None)),
        check_vma=False,
    )
```

```python
import functools

import jax
import jax.numpy as jnp
from jax import lax
from jax.experimental import pallas as pl
from jax.experimental.pallas import tpu as pltpu
from jax.sharding import PartitionSpec as P

f32 = jnp.float32
bf16 = jnp.bfloat16
MESH = pl.DeviceIdType.MESH
VMEM = pl.BlockSpec(memory_space=pltpu.VMEM)
LIMIT = 36 * 2**20


def dot(a, b, flip=False, precision=None):
    dims = (((1,), (1 if flip else 0,)), ((), ()))
    return lax.dot_general(a, b, dims, precision=precision, preferred_element_type=f32)


def split(x):
    high = x.astype(bf16)
    return high, (x - high.astype(f32)).astype(bf16)


def dot3(a, b, flip=False):
    ah, al = split(a)
    bh, bl = split(b)
    return dot(ah, bh, flip) + (dot(ah, bl, flip) + dot(al, bh, flip))


def dot1(a, b):
    return dot(a.astype(bf16), b.astype(bf16))


def full_dot(a, b):
    return dot(a, b, precision=lax.Precision.HIGHEST)


def eye(size):
    rows = lax.broadcasted_iota(jnp.int32, (size, size), 0)
    columns = lax.broadcasted_iota(jnp.int32, (size, size), 1)
    return rows == columns


def scales(pivot):
    only = jnp.where(eye(pivot.shape[0]), pivot, 0.0)
    return (
        lax.rsqrt(jnp.sum(only, axis=1, keepdims=True)),
        lax.rsqrt(jnp.sum(only, axis=0, keepdims=True)),
    )


def row_norm(x):
    return jnp.max(jnp.sum(jnp.abs(x), axis=1, keepdims=True), axis=0, keepdims=True)


def steer(scaled):
    factor = jnp.minimum(1.0, 1.9 / row_norm(scaled))
    rest = jnp.where(eye(scaled.shape[0]), 1.0, 0.0) - factor * scaled
    return factor, rest, row_norm(rest)


def newton(x, rest, steps):
    for _ in range(steps):
        rest = dot1(rest, rest)
        x = x + dot1(x, rest)
    return x


def newton_start(scaled, steps):
    factor, rest, _ = steer(scaled)
    one = jnp.where(eye(scaled.shape[0]), 1.0, 0.0)
    return newton(factor * (one + rest), rest, steps)


def settle(out_ref, a_ref):
    def more(state):
        count, norm = state
        return jnp.logical_and(count < 60, jnp.logical_not(norm < 1e-3))

    def step(state):
        count, _ = state
        one = jnp.where(eye(a_ref.shape[0]), 1.0, 0.0)
        rest = one - full_dot(a_ref[...], out_ref[...])
        out_ref[...] = out_ref[...] + full_dot(out_ref[...], rest)
        return count + 1, row_norm(rest)[0, 0]

    lax.while_loop(more, step, (0, jnp.float32(1.0)))


def begin_kernel(pivot_ref, x_ref, rest_ref, flag_ref, a_ref):
    column, row = scales(pivot_ref[...])
    a_ref[...] = pivot_ref[...] * column * row
    one = jnp.where(eye(a_ref.shape[0]), 1.0, 0.0)
    factor, rest, norm = steer(a_ref[...])
    x_ref[...] = factor * (one + rest)
    rest_ref[...] = rest
    flag_ref[...] = jnp.ones_like(flag_ref)

    @pl.when(jnp.logical_not(norm[0, 0] < 0.7))
    def _():
        x_ref[...] = jnp.where(eye(a_ref.shape[0]), 1.0, 0.0) / row_norm(a_ref[...])
        settle(x_ref, a_ref)
        rest_ref[...] = jnp.zeros_like(rest_ref)
        flag_ref[...] = jnp.zeros_like(flag_ref)


def finish_kernel(pivot_ref, x_ref, out_ref, a_ref):
    column, row = scales(pivot_ref[...])
    a_ref[...] = pivot_ref[...] * column * row
    one = jnp.where(eye(a_ref.shape[0]), 1.0, 0.0)
    x = x_ref[...]
    rest = one - dot3(a_ref[...], x)
    first = row_norm(rest)[0, 0]
    out_ref[...] = x + dot1(x, rest)

    @pl.when(jnp.logical_not(first < 2.0**-7))
    def _():
        @pl.when(jnp.logical_not(first < 0.5))
        def _():
            out_ref[...] = jnp.where(eye(a_ref.shape[0]), 1.0, 0.0) / row_norm(a_ref[...])

        settle(out_ref, a_ref)

    out_ref[...] = out_ref[...] * column * row


def alone(kernel, results, *operands):
    size = operands[0].shape[0]
    return pl.pallas_call(
        kernel,
        out_shape=results,
        in_specs=[VMEM] * len(operands),
        out_specs=jax.tree.map(lambda _: VMEM, results),
        scratch_shapes=[pltpu.VMEM((size, size), f32)],
        compiler_params=pltpu.CompilerParams(vmem_limit_bytes=LIMIT),
    )(*operands)


class Sender:
    def __init__(self, parts, send_sems, recv_sems):
        self.parts, self.send_sems, self.recv_sems = parts, send_sems, recv_sems
        self.count = 0
        self.part = lax.axis_index("tm")
        self.row = lax.axis_index("rows")
        self.copies = []

    def device(self, parts=0, rows=0):
        return (
            lax.rem(self.part + (parts + self.parts), self.parts),
            lax.rem(self.row + (rows + 4), 4),
        )

    def greet(self, *offsets):
        barrier = pltpu.get_barrier_semaphore()
        for parts, rows in offsets:
            pl.semaphore_signal(barrier, inc=1, device_id=self.device(parts, rows), device_id_type=MESH)
        pl.semaphore_wait(barrier, len(offsets))

    def plan(self, source, target, parts=0, rows=0):
        copy = pltpu.make_async_remote_copy(
            src_ref=source,
            dst_ref=target,
            send_sem=self.send_sems.at[self.count],
            recv_sem=self.recv_sems.at[self.count],
            device_id=self.device(parts, rows),
            device_id_type=MESH,
        )
        self.count += 1
        return copy

    def send(self, source, target, parts=0, rows=0):
        copy = self.plan(source, target, parts, rows)
        copy.start()
        self.copies.append(copy)
        return copy

    def sent(self):
        for copy in self.copies:
            copy.wait_send()


class Ring:
    def __init__(self, sender, view):
        row = sender.row
        left, right = lax.rem(row + 3, 4), lax.rem(row + 1, 4)
        self.first = sender.plan(view(row), view(row), rows=1)
        self.second = sender.plan(view(row), view(row), rows=-1)
        self.third = sender.plan(view(left, 0), view(left, 0), rows=1)
        self.fourth = sender.plan(view(right, 1), view(right, 1), rows=-1)

    def start(self):
        self.first.start()
        self.second.start()

    def forward(self):
        self.first.wait_recv()
        self.third.start()
        self.second.wait_recv()
        self.fourth.start()

    def done(self):
        self.third.wait_recv()
        self.fourth.wait_recv()

    def sent(self):
        for copy in (self.first, self.second, self.third, self.fourth):
            copy.wait_send()


def upper(ref, i):
    step = ref.shape[0] // 4
    return ref.at[pl.ds(i * step, step), pl.ds(i * step, (4 - i) * step)]


def mirror(ref):
    step = ref.shape[0] // 4
    for i in range(4):
        for j in range(i + 1, 4):
            here, there = pl.ds(i * step, step), pl.ds(j * step, step)
            ref[there, here] = ref[here, there].T


def columns_of(ref):
    quarter = ref.shape[1] // 4
    half = ref.shape[0] // 2

    def view(q, h=None):
        rows = slice(None) if h is None else pl.ds(h * half, half)
        return ref.at[rows, pl.ds(pl.multiple_of(q * quarter, quarter), quarter)]

    return view


def rows_of(ref):
    quarter = ref.shape[0] // 4
    half = quarter // 2

    def view(q, h=None):
        if h is None:
            return ref.at[pl.ds(pl.multiple_of(q * quarter, quarter), quarter), :]
        return ref.at[pl.ds(pl.multiple_of(q * quarter + h * half, half), half), :]

    return view


def blocks_of(ref):
    half = ref.shape[2] // 2

    def view(q, h=None):
        if h is None:
            return ref.at[q]
        return ref.at[q, :, pl.ds(h * half, half), :]

    return view


def unpack(ref, blocks_ref):
    step = ref.shape[0] // 4

    def place(q):
        return pl.ds(q % 4 * step, step)

    for q in range(4):
        for k in range(3):
            ref[place(q), place(q + k)] = blocks_ref[q, k]
        ref[place(q + 1), place(q)] = blocks_ref[q, 1].T


def second_kernel(
    parts, pivot_ref, lower_ref, s_ref, w_ref, start_ref, rest_ref, flag_ref,
    g_ref, d2_ref, x_ref, v2_ref, u2_ref, left_ref, right_ref, above_left, above_right, below_right,
    wd_ref, su_ref, sdq_ref,
    v_ref, next_ref, w_masked, s_packed, su_blocks, g_below, g_above, v_below, v_above, z_ref, y_ref,
    send_sems, recv_sems,
):
    sender = Sender(parts, send_sems, recv_sems)
    part, row = sender.part, sender.row
    odd = lax.rem(part, 2) == 1
    even = lax.rem(part, 2) == 0
    quarter = lower_ref.shape[1]
    own = pl.ds(pl.multiple_of(row * quarter, quarter), quarter)
    left, right, far = (lax.rem(row + i, 4) for i in (3, 1, 2))
    v_ref[:, own] = jnp.where(part == 0, 0.0, lower_ref[...])
    w_masked[...] = jnp.where(part + 4 >= parts, 0.0, w_ref[...])
    for k in range(3):
        column = pl.multiple_of(lax.rem(row + k, 4) * quarter, quarter)
        s_packed[k] = s_ref[:, pl.ds(column, quarter)]
    view, target = columns_of(v_ref), columns_of(next_ref)
    sender.greet((0, 1), (0, -1), (1, 0), (-1, 0), (2, 0), (-2, 0))

    next_own = sender.send(view(row), target(row), parts=-1)
    ring_v = Ring(sender, view)
    ring_v.start()
    w_own = sender.send(w_masked, rows_of(wd_ref)(row), parts=2)
    su_own = sender.send(s_packed, su_blocks.at[row], parts=-2)

    column, line = scales(pivot_ref[...])
    x_ref[...] = newton(start_ref[...], rest_ref[...], 3)
    rest = dot3(pivot_ref[...] * column * line, x_ref[...])
    rest = jnp.where(eye(rest.shape[0]), 1.0 - rest, -rest) * flag_ref[0:1, 0:1]
    g_ref[...] = (x_ref[...] + dot1(x_ref[...], rest)) * column * line

    from_below = [sender.send(upper(g_ref, i), upper(g_below, i), parts=1) for i in range(4)]
    from_above = [sender.send(upper(g_ref, i), upper(g_above, i), parts=-1) for i in range(4)]
    ring_next = Ring(sender, target)
    passed = [
        sender.plan(view(q, h), target(q, h), parts=-1)
        for q, h in ((left, None), (right, None), (far, 0), (far, 1))
    ]
    v_from_above = sender.plan(next_ref, v_above, parts=-1)

    next_own.wait_recv()

    @pl.when(odd)
    def _():
        ring_next.start()

    ring_v.forward()

    @pl.when(odd)
    def _():
        passed[0].start()
        passed[1].start()

    w_own.wait_recv()
    ring_w = Ring(sender, rows_of(wd_ref))
    ring_w.start()
    su_own.wait_recv()
    ring_u = Ring(sender, blocks_of(su_blocks))
    ring_u.start()

    @pl.when(odd)
    def _():
        ring_next.forward()

    ring_v.done()

    @pl.when(odd)
    def _():
        passed[2].start()
        passed[3].start()

    v_from_below = sender.send(v_ref, v_below, parts=1)
    sd_own = sender.send(s_packed, sdq_ref, parts=2)
    left_ref[...] = dot3(g_ref[...], v_ref[...])

    @pl.when(even)
    def _():
        for copy in passed:
            copy.wait_recv()
        v_from_above.start()

    for copy in from_below:
        copy.wait_recv()
    mirror(g_below)
    y_ref[...] = dot3(v_ref[...], g_below[...])
    d2_ref[...] = pivot_ref[...] - dot3(y_ref[...], v_ref[...], flip=True)
    ring_w.forward()
    below_right[...] = dot3(g_below[own, :], v_ref[...], flip=True)

    @pl.when(odd)
    def _():
        ring_next.done()
        v_from_above.start()

    for copy in from_above:
        copy.wait_recv()
    mirror(g_above)
    z_ref[...] = dot3(next_ref[...].T, g_above[...])
    d2_ref[...] = d2_ref[...] - dot3(z_ref[...], next_ref[...])

    column, line = scales(d2_ref[...])
    x_ref[...] = newton_start(d2_ref[...] * column * line, 3)
    ring_u.forward()
    right_ref[...] = dot3(g_ref[...], next_ref[...], flip=True)
    above_left[...] = dot3(g_above[own, :], next_ref[...])
    v_from_below.wait_recv()
    v2_ref[...] = -dot3(y_ref[...], v_below[...])
    v_from_above.wait_recv()
    u2_ref[...] = -dot3(z_ref[...], v_above[...], flip=True)
    above_right[...] = dot3(g_above[own, :], v_above[...], flip=True)
    sd_own.wait_recv()
    ring_w.done()
    ring_u.done()
    unpack(su_ref, su_blocks)
    sender.sent()
    v_from_above.wait_send()
    for ring in (ring_v, ring_w, ring_u):
        ring.sent()

    @pl.when(odd)
    def _():
        ring_next.sent()
        for copy in passed:
            copy.wait_send()


def third_kernel(
    parts, g2_ref, v2_ref, u2_ref, left_ref, right_ref,
    above_left, above_right, below_right, wd_ref, su_ref, sdq_ref,
    s_out, y_out, down_in, up_in,
    sd_ref, sd_blocks, left2, c_ref, x_ref, y_ref, down_out, up_out,
    xs_out, ys_out, yd_out, xs_in, ys_in, yd_in, send_sems, recv_sems,
):
    sender = Sender(parts, send_sems, recv_sems)
    row = sender.row
    quarter = s_out.shape[0]
    own = pl.ds(pl.multiple_of(row * quarter, quarter), quarter)
    sd_blocks[row] = sdq_ref[...]
    sender.greet((0, 1), (0, -1), (1, 0), (-1, 0), (2, 0), (-2, 0))
    ring_d = Ring(sender, blocks_of(sd_blocks))
    ring_d.start()
    c_ref[...] = dot3(v2_ref[...], wd_ref[...]) + dot3(u2_ref[...], su_ref[...])
    y_ref[...] = dot3(g2_ref[...], c_ref[...])
    ys_out[...] = -dot3(above_left[...], y_ref[...])
    ys = sender.send(ys_out, ys_in, parts=1)
    left2[...] = dot3(g2_ref[...], v2_ref[...])
    down_out[...] = dot3(v2_ref[:, own].T, left2[...])
    from_above = sender.send(down_out, down_in, parts=-2)
    x_ref[...] = dot3(g2_ref[...], u2_ref[...])
    up_out[...] = dot3(u2_ref[:, own].T, x_ref[...])
    from_below = sender.send(up_out, up_in, parts=2)
    x_ref[...] = dot3(u2_ref[...], wd_ref[...], flip=True)
    ring_d.forward()
    x_ref[...] = dot3(x_ref[...], v2_ref[...], flip=True) + dot3(
        c_ref[...], u2_ref[...], flip=True
    )
    c_ref[...] = dot3(g2_ref[...], x_ref[...])
    x_ref[...] = g2_ref[...] + dot3(c_ref[...], g2_ref[...])
    ring_d.done()
    unpack(sd_ref, sd_blocks)
    c_ref[...] = dot3(left2[...], sd_ref[...])
    x_ref[...] = x_ref[...] + dot3(c_ref[...], left2[...], flip=True)
    xs_out[...] = dot3(above_left[...], x_ref[...]) - dot3(above_right[...], y_ref[...], flip=True)
    xs = sender.send(xs_out, xs_in, parts=1)
    yd_out[...] = dot3(below_right[...], x_ref[...])
    yd = sender.send(yd_out, yd_in, parts=-1)

    from_above.wait_recv()
    from_below.wait_recv()
    ys.wait_recv()
    yd.wait_recv()
    y_out[...] = ys_in[...] + yd_in[...]
    s_out[...] = dot3(y_out[...], right_ref[...], flip=True)
    xs.wait_recv()
    s_out[...] = s_out[...] + dot3(xs_in[...], left_ref[...], flip=True)
    sender.sent()
    ring_d.sent()


def local(pivot_blocks, lower_blocks, top_diagonal, top_coupling):
    parts = lax.axis_size("tm")
    size = pivot_blocks.shape[1]
    quarter = lower_blocks.shape[2]
    whole = jax.ShapeDtypeStruct((size, size), f32)
    strip = jax.ShapeDtypeStruct((quarter, size), f32)
    whole_space = pltpu.VMEM((size, size), f32)
    strip_space = pltpu.VMEM((quarter, size), f32)

    def call(kernel, identity, operands, results, scratch, copies):
        return pl.pallas_call(
            functools.partial(kernel, parts),
            out_shape=tuple(results),
            in_specs=[VMEM] * len(operands),
            out_specs=(VMEM,) * len(results),
            scratch_shapes=list(scratch)
            + [pltpu.SemaphoreType.DMA((copies,)), pltpu.SemaphoreType.DMA((copies,))],
            compiler_params=pltpu.CompilerParams(
                collective_id=identity, has_side_effects=True, vmem_limit_bytes=LIMIT
            ),
        )(*operands)

    packed = jax.ShapeDtypeStruct((3, quarter, quarter), f32)
    packed_space = pltpu.VMEM((3, quarter, quarter), f32)
    blocks_space = pltpu.VMEM((4, 3, quarter, quarter), f32)
    pivot = pivot_blocks[0]
    first = alone(begin_kernel, (whole, whole, jax.ShapeDtypeStruct((8, 128), f32)), pivot)
    g, d2, x2, v2, u2, left, right, above_left, above_right, below_right, wd, su, sdq = call(
        second_kernel, 0,
        (pivot, lower_blocks[0], top_diagonal[0], top_coupling[0]) + tuple(first),
        [whole] * 7 + [strip] * 3 + [whole] * 2 + [packed],
        [whole_space] * 2 + [strip_space, packed_space, blocks_space] + [whole_space] * 6, 34,
    )
    g2 = alone(finish_kernel, whole, d2, x2)
    s, y, down, up = call(
        third_kernel, 1,
        (g2, v2, u2, left, right, above_left, above_right, below_right, wd, su, sdq),
        [strip] * 4,
        [whole_space, blocks_space] + [whole_space] * 4 + [strip_space] * 8, 9,
    )
    start = lax.axis_index("rows") * quarter
    s = lax.dynamic_slice_in_dim(g, start, quarter, 0) + s
    reduced = lax.dynamic_slice_in_dim(d2, start, quarter, 0) - down - up
    coupling = jnp.where(lax.axis_index("tm") == parts - 1, 0.0, -y)
    return (s[None], coupling[None], reduced[None])


def solution(mesh):
    placed = (
        P("tm", None, None),
        P("tm", None, "rows"),
        P("tm", "rows", None),
        P("tm", "rows", None),
    )
    return jax.shard_map(
        local,
        mesh=mesh,
        in_specs=placed,
        out_specs=(P("tm", "rows", None), P("tm", "rows", None), P("tm", "rows", None)),
        check_vma=False,
    )
```

```python
import functools

import jax
import jax.numpy as jnp
from jax import lax
from jax.experimental import pallas as pl
from jax.experimental.pallas import tpu as pltpu
from jax.sharding import PartitionSpec as P

f32 = jnp.float32
bf16 = jnp.bfloat16
MESH = pl.DeviceIdType.MESH
VMEM = pl.BlockSpec(memory_space=pltpu.VMEM)
LIMIT = 36 * 2**20


def dot(a, b, flip=False, precision=None):
    dims = (((1,), (1 if flip else 0,)), ((), ()))
    return lax.dot_general(a, b, dims, precision=precision, preferred_element_type=f32)


def split(x):
    high = x.astype(bf16)
    return high, (x - high.astype(f32)).astype(bf16)


def dot3(a, b, flip=False):
    ah, al = split(a)
    bh, bl = split(b)
    return dot(ah, bh, flip) + (dot(ah, bl, flip) + dot(al, bh, flip))


def dot1(a, b):
    return dot(a.astype(bf16), b.astype(bf16))


def full_dot(a, b):
    return dot(a, b, precision=lax.Precision.HIGHEST)


def eye(size):
    rows = lax.broadcasted_iota(jnp.int32, (size, size), 0)
    columns = lax.broadcasted_iota(jnp.int32, (size, size), 1)
    return rows == columns


def scales(pivot):
    only = jnp.where(eye(pivot.shape[0]), pivot, 0.0)
    return (
        lax.rsqrt(jnp.sum(only, axis=1, keepdims=True)),
        lax.rsqrt(jnp.sum(only, axis=0, keepdims=True)),
    )


def row_norm(x):
    return jnp.max(jnp.sum(jnp.abs(x), axis=1, keepdims=True), axis=0, keepdims=True)


def steer(scaled):
    factor = jnp.minimum(1.0, 1.9 / row_norm(scaled))
    rest = jnp.where(eye(scaled.shape[0]), 1.0, 0.0) - factor * scaled
    return factor, rest, row_norm(rest)


def newton(x, rest, steps):
    for _ in range(steps):
        rest = dot1(rest, rest)
        x = x + dot1(x, rest)
    return x


def newton_start(scaled, steps):
    factor, rest, _ = steer(scaled)
    one = jnp.where(eye(scaled.shape[0]), 1.0, 0.0)
    return newton(factor * (one + rest), rest, steps)


def settle(out_ref, a_ref):
    def more(state):
        count, norm = state
        return jnp.logical_and(count < 60, jnp.logical_not(norm < 1e-3))

    def step(state):
        count, _ = state
        one = jnp.where(eye(a_ref.shape[0]), 1.0, 0.0)
        rest = one - full_dot(a_ref[...], out_ref[...])
        out_ref[...] = out_ref[...] + full_dot(out_ref[...], rest)
        return count + 1, row_norm(rest)[0, 0]

    lax.while_loop(more, step, (0, jnp.float32(1.0)))


def begin_kernel(pivot_ref, x_ref, rest_ref, flag_ref, a_ref):
    column, row = scales(pivot_ref[...])
    a_ref[...] = pivot_ref[...] * column * row
    one = jnp.where(eye(a_ref.shape[0]), 1.0, 0.0)
    factor, rest, norm = steer(a_ref[...])
    x_ref[...] = factor * (one + rest)
    rest_ref[...] = rest
    flag_ref[...] = jnp.ones_like(flag_ref)

    @pl.when(jnp.logical_not(norm[0, 0] < 0.7))
    def _():
        x_ref[...] = jnp.where(eye(a_ref.shape[0]), 1.0, 0.0) / row_norm(a_ref[...])
        settle(x_ref, a_ref)
        rest_ref[...] = jnp.zeros_like(rest_ref)
        flag_ref[...] = jnp.zeros_like(flag_ref)


def finish_kernel(pivot_ref, x_ref, out_ref, a_ref):
    column, row = scales(pivot_ref[...])
    a_ref[...] = pivot_ref[...] * column * row
    one = jnp.where(eye(a_ref.shape[0]), 1.0, 0.0)
    x = x_ref[...]
    rest = one - dot3(a_ref[...], x)
    first = row_norm(rest)[0, 0]
    out_ref[...] = x + dot1(x, rest)

    @pl.when(jnp.logical_not(first < 2.0**-7))
    def _():
        @pl.when(jnp.logical_not(first < 0.5))
        def _():
            out_ref[...] = jnp.where(eye(a_ref.shape[0]), 1.0, 0.0) / row_norm(a_ref[...])

        settle(out_ref, a_ref)

    out_ref[...] = out_ref[...] * column * row


def alone(kernel, results, *operands):
    size = operands[0].shape[0]
    return pl.pallas_call(
        kernel,
        out_shape=results,
        in_specs=[VMEM] * len(operands),
        out_specs=jax.tree.map(lambda _: VMEM, results),
        scratch_shapes=[pltpu.VMEM((size, size), f32)],
        compiler_params=pltpu.CompilerParams(vmem_limit_bytes=LIMIT),
    )(*operands)


class Sender:
    def __init__(self, parts, send_sems, recv_sems):
        self.parts, self.send_sems, self.recv_sems = parts, send_sems, recv_sems
        self.count = 0
        self.part = lax.axis_index("tm")
        self.row = lax.axis_index("rows")
        self.copies = []

    def device(self, parts=0, rows=0):
        return (
            lax.rem(self.part + (parts + self.parts), self.parts),
            lax.rem(self.row + (rows + 4), 4),
        )

    def greet(self, *offsets):
        barrier = pltpu.get_barrier_semaphore()
        for parts, rows in offsets:
            pl.semaphore_signal(barrier, inc=1, device_id=self.device(parts, rows), device_id_type=MESH)
        pl.semaphore_wait(barrier, len(offsets))

    def plan(self, source, target, parts=0, rows=0):
        copy = pltpu.make_async_remote_copy(
            src_ref=source,
            dst_ref=target,
            send_sem=self.send_sems.at[self.count],
            recv_sem=self.recv_sems.at[self.count],
            device_id=self.device(parts, rows),
            device_id_type=MESH,
        )
        self.count += 1
        return copy

    def send(self, source, target, parts=0, rows=0):
        copy = self.plan(source, target, parts, rows)
        copy.start()
        self.copies.append(copy)
        return copy

    def sent(self):
        for copy in self.copies:
            copy.wait_send()


class Ring:
    def __init__(self, sender, view):
        row = sender.row
        left, right = lax.rem(row + 3, 4), lax.rem(row + 1, 4)
        self.first = sender.plan(view(row), view(row), rows=1)
        self.second = sender.plan(view(row), view(row), rows=-1)
        self.third = sender.plan(view(left, 0), view(left, 0), rows=1)
        self.fourth = sender.plan(view(right, 1), view(right, 1), rows=-1)

    def start(self):
        self.first.start()
        self.second.start()

    def forward(self):
        self.first.wait_recv()
        self.third.start()
        self.second.wait_recv()
        self.fourth.start()

    def done(self):
        self.third.wait_recv()
        self.fourth.wait_recv()

    def sent(self):
        for copy in (self.first, self.second, self.third, self.fourth):
            copy.wait_send()


def upper(ref, i):
    step = ref.shape[0] // 4
    return ref.at[pl.ds(i * step, step), pl.ds(i * step, (4 - i) * step)]


def mirror(ref):
    step = ref.shape[0] // 4
    for i in range(4):
        for j in range(i + 1, 4):
            here, there = pl.ds(i * step, step), pl.ds(j * step, step)
            ref[there, here] = ref[here, there].T


def columns_of(ref):
    quarter = ref.shape[1] // 4
    half = ref.shape[0] // 2

    def view(q, h=None):
        rows = slice(None) if h is None else pl.ds(h * half, half)
        return ref.at[rows, pl.ds(pl.multiple_of(q * quarter, quarter), quarter)]

    return view


def rows_of(ref):
    quarter = ref.shape[0] // 4
    half = quarter // 2

    def view(q, h=None):
        if h is None:
            return ref.at[pl.ds(pl.multiple_of(q * quarter, quarter), quarter), :]
        return ref.at[pl.ds(pl.multiple_of(q * quarter + h * half, half), half), :]

    return view


def blocks_of(ref):
    half = ref.shape[2] // 2

    def view(q, h=None):
        if h is None:
            return ref.at[q]
        return ref.at[q, :, pl.ds(h * half, half), :]

    return view


def unpack(ref, blocks_ref):
    step = ref.shape[0] // 4

    def place(q):
        return pl.ds(q % 4 * step, step)

    for q in range(4):
        for k in range(3):
            ref[place(q), place(q + k)] = blocks_ref[q, k]
        ref[place(q + 1), place(q)] = blocks_ref[q, 1].T


def second_kernel(
    parts, pivot_ref, lower_ref, s_ref, w_ref, start_ref, rest_ref, flag_ref,
    g_ref, d2_ref, x_ref, v2_ref, u2_ref, left_ref, right_ref, above_left, above_right, below_right,
    wd_ref, su_ref, sdq_ref,
    v_ref, next_ref, w_masked, s_packed, su_blocks, g_below, g_above, v_below, v_above, z_ref, y_ref,
    send_sems, recv_sems,
):
    sender = Sender(parts, send_sems, recv_sems)
    part, row = sender.part, sender.row
    odd = lax.rem(part, 2) == 1
    even = lax.rem(part, 2) == 0
    quarter = lower_ref.shape[1]
    own = pl.ds(pl.multiple_of(row * quarter, quarter), quarter)
    left, right, far = (lax.rem(row + i, 4) for i in (3, 1, 2))
    v_ref[:, own] = jnp.where(part == 0, 0.0, lower_ref[...])
    w_masked[...] = jnp.where(part + 4 >= parts, 0.0, w_ref[...])
    for k in range(3):
        column = pl.multiple_of(lax.rem(row + k, 4) * quarter, quarter)
        s_packed[k] = s_ref[:, pl.ds(column, quarter)]
    view, target = columns_of(v_ref), columns_of(next_ref)
    sender.greet((0, 1), (0, -1), (1, 0), (-1, 0), (2, 0), (-2, 0))

    next_own = sender.send(view(row), target(row), parts=-1)
    ring_v = Ring(sender, view)
    ring_v.start()
    w_own = sender.send(w_masked, rows_of(wd_ref)(row), parts=2)
    su_own = sender.send(s_packed, su_blocks.at[row], parts=-2)

    column, line = scales(pivot_ref[...])
    x_ref[...] = newton(start_ref[...], rest_ref[...], 3)
    rest = dot3(pivot_ref[...] * column * line, x_ref[...])
    rest = jnp.where(eye(rest.shape[0]), 1.0 - rest, -rest) * flag_ref[0:1, 0:1]
    g_ref[...] = (x_ref[...] + dot1(x_ref[...], rest)) * column * line

    from_below = [sender.send(upper(g_ref, i), upper(g_below, i), parts=1) for i in range(4)]
    from_above = [sender.send(upper(g_ref, i), upper(g_above, i), parts=-1) for i in range(4)]
    ring_next = Ring(sender, target)
    passed = [
        sender.plan(view(q, h), target(q, h), parts=-1)
        for q, h in ((left, None), (right, None), (far, 0), (far, 1))
    ]
    v_from_above = sender.plan(next_ref, v_above, parts=-1)

    next_own.wait_recv()

    @pl.when(odd)
    def _():
        ring_next.start()

    ring_v.forward()

    @pl.when(odd)
    def _():
        passed[0].start()
        passed[1].start()

    w_own.wait_recv()
    ring_w = Ring(sender, rows_of(wd_ref))
    ring_w.start()
    su_own.wait_recv()
    ring_u = Ring(sender, blocks_of(su_blocks))
    ring_u.start()

    @pl.when(odd)
    def _():
        ring_next.forward()

    ring_v.done()

    @pl.when(odd)
    def _():
        passed[2].start()
        passed[3].start()

    v_from_below = sender.send(v_ref, v_below, parts=1)
    sd_own = sender.send(s_packed, sdq_ref, parts=2)
    left_ref[...] = dot3(g_ref[...], v_ref[...])

    @pl.when(even)
    def _():
        for copy in passed:
            copy.wait_recv()
        v_from_above.start()

    for copy in from_below:
        copy.wait_recv()
    mirror(g_below)
    y_ref[...] = dot3(v_ref[...], g_below[...])
    d2_ref[...] = pivot_ref[...] - dot3(y_ref[...], v_ref[...], flip=True)
    ring_w.forward()
    below_right[...] = dot3(g_below[own, :], v_ref[...], flip=True)

    @pl.when(odd)
    def _():
        ring_next.done()
        v_from_above.start()

    for copy in from_above:
        copy.wait_recv()
    mirror(g_above)
    z_ref[...] = dot3(next_ref[...].T, g_above[...])
    d2_ref[...] = d2_ref[...] - dot3(z_ref[...], next_ref[...])

    column, line = scales(d2_ref[...])
    x_ref[...] = newton_start(d2_ref[...] * column * line, 3)
    ring_u.forward()
    right_ref[...] = dot3(g_ref[...], next_ref[...], flip=True)
    above_left[...] = dot3(g_above[own, :], next_ref[...])
    v_from_below.wait_recv()
    v2_ref[...] = -dot3(y_ref[...], v_below[...])
    v_from_above.wait_recv()
    u2_ref[...] = -dot3(z_ref[...], v_above[...], flip=True)
    above_right[...] = dot3(g_above[own, :], v_above[...], flip=True)
    sd_own.wait_recv()
    ring_w.done()
    ring_u.done()
    unpack(su_ref, su_blocks)
    sender.sent()
    v_from_above.wait_send()
    for ring in (ring_v, ring_w, ring_u):
        ring.sent()

    @pl.when(odd)
    def _():
        ring_next.sent()
        for copy in passed:
            copy.wait_send()


def third_kernel(
    parts, g2_ref, v2_ref, u2_ref, left_ref, right_ref,
    above_left, above_right, below_right, wd_ref, su_ref, sdq_ref,
    s_out, y_out, down_in, up_in,
    sd_ref, sd_blocks, left2, c_ref, x_ref, y_ref, down_out, up_out,
    xs_out, ys_out, yd_out, xs_in, ys_in, yd_in, send_sems, recv_sems,
):
    sender = Sender(parts, send_sems, recv_sems)
    row = sender.row
    quarter = s_out.shape[0]
    own = pl.ds(pl.multiple_of(row * quarter, quarter), quarter)
    sd_blocks[row] = sdq_ref[...]
    sender.greet((0, 1), (0, -1), (1, 0), (-1, 0), (2, 0), (-2, 0))
    ring_d = Ring(sender, blocks_of(sd_blocks))
    ring_d.start()
    c_ref[...] = dot3(v2_ref[...], wd_ref[...]) + dot3(u2_ref[...], su_ref[...])
    y_ref[...] = dot3(g2_ref[...], c_ref[...])
    ys_out[...] = -dot3(above_left[...], y_ref[...])
    ys = sender.send(ys_out, ys_in, parts=1)
    left2[...] = dot3(g2_ref[...], v2_ref[...])
    down_out[...] = dot3(v2_ref[:, own].T, left2[...])
    from_above = sender.send(down_out, down_in, parts=-2)
    up_out[...] = dot3(dot3(u2_ref[:, own].T, g2_ref[...]), u2_ref[...])
    from_below = sender.send(up_out, up_in, parts=2)
    x_ref[...] = dot3(u2_ref[...], wd_ref[...], flip=True)
    ring_d.forward()
    x_ref[...] = dot3(x_ref[...], v2_ref[...], flip=True) + dot3(
        c_ref[...], u2_ref[...], flip=True
    )
    c_ref[...] = dot3(g2_ref[...], x_ref[...])
    x_ref[...] = g2_ref[...] + dot3(c_ref[...], g2_ref[...])
    ring_d.done()
    unpack(sd_ref, sd_blocks)
    c_ref[...] = dot3(left2[...], sd_ref[...])
    x_ref[...] = x_ref[...] + dot3(c_ref[...], left2[...], flip=True)
    xs_out[...] = dot3(above_left[...], x_ref[...]) - dot3(above_right[...], y_ref[...], flip=True)
    xs = sender.send(xs_out, xs_in, parts=1)
    yd_out[...] = dot3(below_right[...], x_ref[...])
    yd = sender.send(yd_out, yd_in, parts=-1)

    from_above.wait_recv()
    from_below.wait_recv()
    ys.wait_recv()
    yd.wait_recv()
    y_out[...] = ys_in[...] + yd_in[...]
    s_out[...] = dot3(y_out[...], right_ref[...], flip=True)
    xs.wait_recv()
    s_out[...] = s_out[...] + dot3(xs_in[...], left_ref[...], flip=True)
    sender.sent()
    ring_d.sent()


def local(pivot_blocks, lower_blocks, top_diagonal, top_coupling):
    parts = lax.axis_size("tm")
    size = pivot_blocks.shape[1]
    quarter = lower_blocks.shape[2]
    whole = jax.ShapeDtypeStruct((size, size), f32)
    strip = jax.ShapeDtypeStruct((quarter, size), f32)
    whole_space = pltpu.VMEM((size, size), f32)
    strip_space = pltpu.VMEM((quarter, size), f32)

    def call(kernel, identity, operands, results, scratch, copies):
        return pl.pallas_call(
            functools.partial(kernel, parts),
            out_shape=tuple(results),
            in_specs=[VMEM] * len(operands),
            out_specs=(VMEM,) * len(results),
            scratch_shapes=list(scratch)
            + [pltpu.SemaphoreType.DMA((copies,)), pltpu.SemaphoreType.DMA((copies,))],
            compiler_params=pltpu.CompilerParams(
                collective_id=identity, has_side_effects=True, vmem_limit_bytes=LIMIT
            ),
        )(*operands)

    packed = jax.ShapeDtypeStruct((3, quarter, quarter), f32)
    packed_space = pltpu.VMEM((3, quarter, quarter), f32)
    blocks_space = pltpu.VMEM((4, 3, quarter, quarter), f32)
    pivot = pivot_blocks[0]
    first = alone(begin_kernel, (whole, whole, jax.ShapeDtypeStruct((8, 128), f32)), pivot)
    g, d2, x2, v2, u2, left, right, above_left, above_right, below_right, wd, su, sdq = call(
        second_kernel, 0,
        (pivot, lower_blocks[0], top_diagonal[0], top_coupling[0]) + tuple(first),
        [whole] * 7 + [strip] * 3 + [whole] * 2 + [packed],
        [whole_space] * 2 + [strip_space, packed_space, blocks_space] + [whole_space] * 6, 34,
    )
    g2 = alone(finish_kernel, whole, d2, x2)
    s, y, down, up = call(
        third_kernel, 1,
        (g2, v2, u2, left, right, above_left, above_right, below_right, wd, su, sdq),
        [strip] * 4,
        [whole_space, blocks_space] + [whole_space] * 4 + [strip_space] * 8, 9,
    )
    start = lax.axis_index("rows") * quarter
    s = lax.dynamic_slice_in_dim(g, start, quarter, 0) + s
    reduced = lax.dynamic_slice_in_dim(d2, start, quarter, 0) - down - up
    coupling = jnp.where(lax.axis_index("tm") == parts - 1, 0.0, -y)
    return (s[None], coupling[None], reduced[None])


def solution(mesh):
    placed = (
        P("tm", None, None),
        P("tm", None, "rows"),
        P("tm", "rows", None),
        P("tm", "rows", None),
    )
    return jax.shard_map(
        local,
        mesh=mesh,
        in_specs=placed,
        out_specs=(P("tm", "rows", None), P("tm", "rows", None), P("tm", "rows", None)),
        check_vma=False,
    )
```
